512 devices in a mesh: dp: 4 (over x), tensor: 8 (over y, core), pipe: 16 (over z).
Axes of the slice: x: 4, y: 4, z: 16, core: 2. Of those that a mesh axis runs over, the one named last changes fastest.
Arguments:
- tokens: bfloat16 [1024, 4096], P(('dp', 'pipe'), 'tensor'), parts along dimension 0, may hold values from -6 to 6
- final_gain: float32 [4096], replicated, may hold values from 0.5 to 1.5
- unembed: bfloat16 [76800, 4096], P(('tensor', 'pipe')), may hold values from -0.28125 to 0.28125
- targets: int32 [1024], P('dp'), parts along dimension 0, may hold values from 0 to 76799
Outputs:
- row_loss: float32 [1024], P('dp'), parts along dimension 0
- tokens_grad: float32 [1024, 4096], P(('dp', 'pipe'), 'tensor'), parts along dimension 0
The draws below stay inside these ranges and needn't reach their ends.
There are 4 independent parts, one for each index of `dp`. The reference program is written for one: setup_inputs(seed, part) draws one part's arguments, and reference() takes and returns one part's arrays. A program takes and returns all parts, laid end to end along the dimension named above; an argument that names none is the same for every part. Nothing has to cross between parts.
All inputs are finite; a program needn't handle non-finite values.
Results may differ from the reference program's by a relative error of at most 0.0045.
Values may be sent and summed in bfloat16 or wider, within the bound.
A program may use at most 64 MiB of HBM per device.

```python
import math
import jax
import jax.numpy as jnp
import numpy as np
from jax import lax

D = 4096
VOCAB = 76800
ROWS = 256


def draw_tokens(key, part):
    key = jax.random.fold_in(key, 11)
    values = jnp.clip(jax.random.normal(key, (ROWS, D), jnp.float32), -6.0, 6.0)
    return values.astype(jnp.bfloat16)


def draw_unembed(key, part):
    key = jax.random.fold_in(key, 23)
    spread = 3.0 / math.sqrt(D)
    values = jnp.clip(jax.random.normal(key, (VOCAB, D), jnp.float32), -6.0, 6.0) * spread
    return values.astype(jnp.bfloat16)


def plant(entries, key, smallest, top_value):
    spot = [jax.random.randint(jax.random.fold_in(key, axis), (), 0, length) for axis, length in enumerate(entries.shape)]
    widest = entries.shape.index(max(entries.shape))
    neighbour = spot[:widest] + [(spot[widest] + 1) % entries.shape[widest]] + spot[widest + 1:]
    return entries.at[tuple(spot)].set(smallest).at[tuple(neighbour)].set(top_value)


def skewed_wide(rng, shape, number_of, slope):
    weights = [min(1 << octave, number_of + 1 - (1 << octave)) * (1 << 20) // math.isqrt((1 << octave) ** slope) + 1 for octave in range((number_of + 1).bit_length()) if 1 << octave <= number_of]
    scale = 1 + sum(weights) // (1 << 30)
    listing = np.cumsum(np.array([max(1, weight // scale) for weight in weights]))
    ticket = jax.random.randint(jax.random.fold_in(rng, 1), shape, 0, int(listing[len(weights) - 1]))
    start = jnp.left_shift(1, jnp.searchsorted(jnp.asarray(listing, jnp.int32), ticket, side="right").astype(jnp.int32))
    rank = start - 1 + jax.random.randint(jax.random.fold_in(rng, 4), shape, 0, 1 << 30) % jnp.minimum(start, number_of + 1 - start)
    return jax.random.permutation(jax.random.fold_in(rng, 2), number_of)[rank].astype(jnp.int32)


def setup_inputs(seed: int = 0, part: int = 0) -> dict:
    splits = jax.random.split(jax.random.key(seed), 5)
    part_keys = jax.random.split(jax.random.fold_in(splits[4], part), 5)
    tokens = draw_tokens(jax.random.fold_in(jax.random.fold_in(splits[4], part), 71), part)
    final_gain = jnp.clip(1.0 + 0.1 * jax.random.normal(splits[1], (D,), jnp.float32), 0.5, 1.5)
    unembed = draw_unembed(jax.random.fold_in(splits[4], 71), part)
    targets = plant(skewed_wide(part_keys[3], (ROWS,), VOCAB, 2), jax.random.fold_in(part_keys[3], 3), 0, VOCAB - 1).astype(jnp.int32)
    return {"tokens": tokens, "final_gain": final_gain, "unembed": unembed, "targets": targets}


EPS = 1e-06

def reference(tokens, final_gain, unembed, targets):
    stream = tokens.astype(jnp.float32)
    inv_rms = lax.rsqrt(lax.optimization_barrier(jnp.mean(stream * stream, axis=1, keepdims=True)) + EPS)
    final = (stream * inv_rms * final_gain[None, :]).astype(jnp.bfloat16)
    dims = (((1,), (1,)), ((), ()))
    logits = lax.dot_general(final, unembed, dims, preferred_element_type=jnp.float32)
    row_top = lax.optimization_barrier(jnp.max(logits, axis=1, keepdims=True))
    exp_total = lax.optimization_barrier(jnp.sum(jnp.exp(logits - row_top), axis=1, keepdims=True))
    log_total = row_top + jnp.log(exp_total)
    picked = jnp.take_along_axis(logits, targets[:, None].astype(jnp.int32), axis=1)
    row_loss = (log_total - picked)[:, 0]
    vocab_ids = jnp.arange(logits.shape[1], dtype=jnp.int32)
    onehot = (vocab_ids[None, :] == targets[:, None]).astype(jnp.float32)
    probs_diff = (jnp.exp(logits - log_total) - onehot).astype(jnp.bfloat16)
    final_grad = jnp.dot(probs_diff, unembed, preferred_element_type=jnp.float32)
    weighted = final_grad * final_gain[None, :]
    dots = lax.optimization_barrier(jnp.mean(weighted * stream, axis=1, keepdims=True))
    tokens_grad = inv_rms * (weighted - stream * (inv_rms * inv_rms * dots))
    return (row_loss, tokens_grad)
```

```python
import functools

import jax
import jax.numpy as jnp
from jax import lax
from jax.experimental import pallas as pl
from jax.experimental.pallas import tpu as pltpu
from jax.sharding import PartitionSpec as P

EPS = 1e-06
MESH = pl.DeviceIdType.MESH
NY, NC, NZ = 4, 2, 16
NT = NY * NC
BLK = 16
F32, BF16 = jnp.float32, jnp.bfloat16
GROUPS = [[(0, 1)], [(1, 2), (14, 2)], [(3, 2), (12, 2)], [(5, 7)]]
Z_ORDER = [8, 7, 9, 6, 10, 5, 11, 4, 12, 3, 13, 2, 14, 1, 15]
Y_ORDER = [2, 1, 3]


def kernel(
    tok_ref, gain_ref, tgt_ref, u_hbm, loss_ref, grad_ref,
    xs, us, ug, logits, q, term, send_t, send_o, core_t, core_o, y_t, y_o, own, z_send, z_recv,
    stat_send, stat_y, group, stat_z, twice, twice_int, u_sem, send_sem, recv_sem,
):
    dp = lax.axis_index("dp")
    t = lax.axis_index("tensor")
    z = lax.axis_index("pipe")
    y, c = t // NC, t % NC
    rows = BLK * NZ
    width = tok_ref.shape[1]
    vocab = us.shape[1]
    count = [0]
    started = []

    def tensor_of(dy, dc):
        return lax.rem(y + dy, NY) * NC + lax.rem(c + dc, NC)

    def at_tensor(dy, dc):
        return (dp, tensor_of(dy, dc), z)

    def at_pipe(d):
        return (dp, t, lax.rem(z + d, NZ))

    def send(src, dst, device):
        i = count[0]
        count[0] += 1
        copy = pltpu.make_async_remote_copy(
            src_ref=src, dst_ref=dst, send_sem=send_sem.at[i], recv_sem=recv_sem.at[i],
            device_id=device, device_id_type=MESH,
        )
        copy.start()
        started.append(copy)
        return copy

    barrier = pltpu.get_barrier_semaphore()
    for d in range(1, NZ):
        pl.semaphore_signal(barrier, inc=1, device_id=at_pipe(d), device_id_type=MESH)
    for j in range(1, NT):
        pl.semaphore_signal(barrier, inc=1, device_id=at_tensor(j // NC, j % NC), device_id_type=MESH)

    loads = []
    for k in range(NT):
        load = pltpu.make_async_copy(u_hbm.at[:, pl.ds(k * width, width)], us.at[k], u_sem.at[k])
        load.start()
        loads.append(load)
    own_copy = pltpu.make_async_copy(tok_ref, xs.at[t, pl.ds(0, BLK)], u_sem.at[NT])
    own_copy.start()

    for h in range(2):
        part = jnp.transpose(jnp.broadcast_to(tgt_ref[h : h + 1, :], (128, 128)))
        twice_int[pl.ds(h * 128, 128), :] = part
        twice_int[pl.ds(rows + h * 128, 128), :] = part
    shift = pl.multiple_of(z * BLK, BLK)
    back = pl.multiple_of(rows - z * BLK, BLK)
    vocab_start = (t * NZ + z) * vocab
    own_copy.wait()

    pl.semaphore_wait(barrier, NZ - 1 + NT - 1)

    z_copies = {}
    for d in Z_ORDER:
        z_copies[d] = send(tok_ref, xs.at[t, pl.ds((NZ - d) * BLK, BLK)], at_pipe(d))
    y_copies, core_own = [], []

    def forward(g):
        for first, number in GROUPS[g]:
            piece = xs.at[t, pl.ds(first * BLK, number * BLK)]
            for dy in Y_ORDER:
                y_copies.append((g, dy, first, number, send(piece, piece, at_tensor(dy, 0))))
            core_own.append(send(piece, piece, at_tensor(0, 1)))

    core_far = []

    def hand_over(g):
        for group_of, dy, first, number, copy in y_copies:
            if group_of == g:
                copy.wait_recv()
                source = tensor_of(NY - dy, 0)
                piece = xs.at[source, pl.ds(first * BLK, number * BLK)]
                core_far.append(send(piece, piece, at_tensor(0, 1)))

    def wait_group(g):
        for first, number in GROUPS[g]:
            for s in range(first, first + number):
                z_copies[NZ - s].wait_recv()

    forward(0)
    for k in range(NT):
        loads[k].wait()

    def scale_u(k, _):
        ug[k] = (us[k].astype(F32) * gain_ref[pl.ds(k, 1), :]).astype(BF16)
        return 0

    lax.fori_loop(0, NT, scale_u, 0)
    wait_group(1)
    forward(1)
    hand_over(0)

    lane = lax.broadcasted_iota(jnp.int32, (rows, vocab), 1)
    local = twice_int[pl.ds(shift, rows), :] - vocab_start
    local5 = jnp.concatenate([local] * 5, axis=1)[:, :vocab]
    onehot = (lane == local5).astype(F32).astype(BF16)
    q[...] = onehot

    def pick_row(k, _):
        send_o[k] = jnp.dot(q[...], us[k], preferred_element_type=F32).astype(BF16)
        return 0

    lax.fori_loop(0, NT, pick_row, 0)
    wait_group(2)
    forward(2)
    hand_over(1)
    wait_group(3)
    forward(3)
    o_core = []
    for dy in range(NY):
        o_core.append(send(send_o.at[tensor_of(dy, 1)], core_o.at[dy], at_tensor(0, 1)))
    hand_over(2)
    o_y = {}
    for dy in Y_ORDER + [0]:
        o_core[dy].wait_recv()
        mine = tensor_of(dy, 0)
        send_o[mine] = (send_o[mine].astype(F32) + core_o[dy].astype(F32)).astype(BF16)
        if dy:
            o_y[dy] = send(send_o.at[mine], y_o.at[dy - 1], at_tensor(dy, 0))
    hand_over(3)
    for copy in core_own + core_far:
        copy.wait_recv()

    logits[...] = jnp.zeros_like(logits)

    def multiply(k, total):
        x = xs[k]
        logits[...] += lax.dot_general(x, ug[k], (((1,), (1,)), ((), ())), preferred_element_type=F32)
        xf = x.astype(F32)
        xf = xf * xf
        for i in range(width // 128):
            total = total + xf[:, i * 128 : (i + 1) * 128]
        return total

    squares = lax.fori_loop(0, NT, multiply, jnp.zeros((rows, 128), F32))
    inv = lax.rsqrt(jnp.sum(squares, axis=1, keepdims=True) / (width * NT) + EPS)
    own_inv = inv[:BLK]
    twice[pl.ds(0, rows), :] = jnp.broadcast_to(inv, (rows, 128))
    lane_id = lax.broadcasted_iota(jnp.int32, (64, 128), 1)
    column = lax.broadcasted_iota(jnp.int32, (64, vocab), 1)
    for r in range(0, rows, 64):
        part = pl.ds(r, 64)
        l = logits[part, :] * twice[part, :][:, :1]
        tgt = twice_int[pl.ds(pl.multiple_of(shift + r, BLK), 64), :][:, :1] - vocab_start
        here = column == tgt
        top = jnp.max(l, axis=1, keepdims=True)
        e = jnp.where(here, 0.0, jnp.exp(l - top))
        q[part, :] = e.astype(BF16)
        total = jnp.sum(e, axis=1, keepdims=True)
        mixed = jnp.sum(e * l, axis=1, keepdims=True)
        picked = jnp.sum(jnp.where(here, l, 0.0), axis=1, keepdims=True)
        stats = jnp.where(lane_id == 0, top, jnp.where(lane_id == 1, total, jnp.where(lane_id == 2, mixed, picked)))
        twice[part, :] = stats
        twice[pl.ds(rows + r, 64), :] = stats
    for h in range(2):
        across = jnp.transpose(twice[pl.ds(pl.multiple_of(back + h * 128, BLK), 128), :]) if h == 0 else jnp.transpose(
            twice[pl.ds(pl.multiple_of(lax.rem(back + h * 128, rows), BLK), 128), :])
        for i in range(4):
            stat_send[pl.ds(2 * i + h, 1), :] = across[i : i + 1, :]
    y_stats = []
    for j in range(1, NT):
        y_stats.append(send(stat_send, stat_y.at[j], at_tensor(j // NC, j % NC)))

    def gradient(k, _):
        term[k] = jnp.dot(q[...], us[k], preferred_element_type=F32)
        return 0

    lax.fori_loop(0, NT, gradient, 0)

    def merge(tiles):
        top = tiles[0][0:2]
        for tile in tiles[1:]:
            top = jnp.maximum(top, tile[0:2])
        total = mixed = picked = jnp.zeros((2, 128), F32)
        for tile in tiles:
            factor = jnp.exp(tile[0:2] - top)
            total = total + factor * tile[2:4]
            mixed = mixed + factor * tile[4:6]
            picked = picked + tile[6:8]
        return top, total, mixed, picked

    def spread(value):
        for h in range(2):
            part = jnp.transpose(jnp.broadcast_to(value[h : h + 1, :], (128, 128)))
            twice[pl.ds(h * 128, 128), :] = part
            twice[pl.ds(rows + h * 128, 128), :] = part
        return twice[pl.ds(shift, rows), :]

    for copy in y_stats:
        copy.wait_recv()
    mine = stat_send[...]
    top, total, mixed, picked = merge([mine] + [stat_y[j] for j in range(1, NT)])
    group[0:2, :] = top
    group[2:4, :] = total
    group[4:6, :] = mixed
    group[6:8, :] = picked
    z_stats = []
    for d in Z_ORDER:
        z_stats.append(send(group, stat_z.at[d], at_pipe(d)))
    factor = spread(jnp.exp(mine[0:2] - top))
    factor4 = jnp.concatenate([factor] * (width // 128), axis=1)

    def rounded(k, _):
        send_t[k] = (term[k] * factor4).astype(BF16)
        return 0

    lax.fori_loop(0, NT, rounded, 0)
    t_core = {}
    for dy in Y_ORDER + [0]:
        t_core[dy] = send(send_t.at[tensor_of(dy, 1)], core_t.at[dy], at_tensor(0, 1))
    t_y = {}
    far, near = [(4, 8)], [(12, 4), (0, 4)]
    for dy in Y_ORDER:
        t_core[dy].wait_recv()
        k = tensor_of(dy, 0)
        send_t[k] = (send_t[k].astype(F32) + core_t[dy].astype(F32)).astype(BF16)
        for first, number in far + near:
            piece = pl.ds(first * BLK, number * BLK)
            t_y[dy, first] = send(send_t.at[k, piece], y_t.at[dy - 1, piece], at_tensor(dy, 0))
    t_core[0].wait_recv()
    for dy in Y_ORDER:
        o_y[dy].wait_recv()
    for copy in z_stats:
        copy.wait_recv()
    group_top = group[0:2]
    top, total, mixed, picked = merge([group[...]] + [stat_z[d] for d in range(1, NZ)])
    at_target = jnp.exp(picked - top)
    full = total + at_target
    loss_ref[...] = top + jnp.log(full) - picked
    kept = total / full
    scale = spread(jnp.exp(group_top - top) / full)
    own[...] = scale
    drop = spread(kept)
    own_dot = spread((mixed - total * picked) / full)[:BLK]
    z_grads = {}
    for part_of in (far, near):
        for first, number in part_of:
            piece = pl.ds(first * BLK, number * BLK)
            for dy in Y_ORDER:
                t_y[dy, first].wait_recv()
            value = send_t[t, piece, :].astype(F32) + core_t[0, piece, :].astype(F32)
            target = send_o[t, piece, :].astype(F32)
            for dy in range(NY - 1):
                value = value + y_t[dy, piece, :].astype(F32)
                target = target + y_o[dy, piece, :].astype(F32)
            a = own[piece, :]
            b = drop[first * BLK : (first + number) * BLK]
            for i in range(width // 128):
                cut = slice(i * 128, (i + 1) * 128)
                v = value[:, cut] * a - target[:, cut] * b
                z_send[piece, cut] = v.astype(BF16)
                if first == 0:
                    term[0, pl.ds(0, BLK), cut] = v[:BLK]
        for d in Z_ORDER:
            if any(first <= d < first + number for first, number in part_of):
                z_grads[d] = send(z_send.at[pl.ds(d * BLK, BLK)], z_recv.at[d], at_pipe(d))
    grad = term[0, pl.ds(0, BLK), :]
    for d in reversed(Z_ORDER):
        z_grads[d].wait_recv()
        grad = grad + z_recv[d].astype(F32)
    stream = tok_ref[...].astype(F32)
    weighted = grad * gain_ref[pl.ds(t, 1), :]
    dots = own_dot[:, :1] / (own_inv * (width * NT))
    grad_ref[...] = own_inv * (weighted - stream * (own_inv * own_inv * dots))
    for copy in started:
        copy.wait_send()


def body(tokens, final_gain, unembed, targets):
    vocab, features = unembed.shape
    width = tokens.shape[1]
    rows = targets.shape[0]
    vmem = pl.BlockSpec(memory_space=pltpu.VMEM)
    loss, grad = pl.pallas_call(
        kernel,
        out_shape=(
            jax.ShapeDtypeStruct((2, 128), F32),
            jax.ShapeDtypeStruct(tokens.shape, F32),
        ),
        in_specs=[vmem, vmem, vmem, pl.BlockSpec(memory_space=pl.ANY)],
        out_specs=(vmem, vmem),
        scratch_shapes=[
            pltpu.VMEM((NT, rows, width), BF16),
            pltpu.VMEM((NT, vocab, width), BF16),
            pltpu.VMEM((NT, vocab, width), BF16),
            pltpu.VMEM((rows, vocab), F32),
            pltpu.VMEM((rows, vocab), BF16),
            pltpu.VMEM((NT, rows, width), F32),
            pltpu.VMEM((NT, rows, width), BF16),
            pltpu.VMEM((NT, rows, width), BF16),
            pltpu.VMEM((NY, rows, width), BF16),
            pltpu.VMEM((NY, rows, width), BF16),
            pltpu.VMEM((NY - 1, rows, width), BF16),
            pltpu.VMEM((NY - 1, rows, width), BF16),
            pltpu.VMEM((rows, 128), F32),
            pltpu.VMEM((rows, width), BF16),
            pltpu.VMEM((NZ, BLK, width), BF16),
            pltpu.VMEM((8, 128), F32),
            pltpu.VMEM((NT, 8, 128), F32),
            pltpu.VMEM((8, 128), F32),
            pltpu.VMEM((NZ, 8, 128), F32),
            pltpu.VMEM((2 * rows, 128), F32),
            pltpu.VMEM((2 * rows, 128), jnp.int32),
            pltpu.SemaphoreType.DMA((NT + 1,)),
            pltpu.SemaphoreType.DMA((160,)),
            pltpu.SemaphoreType.DMA((160,)),
        ],
        compiler_params=pltpu.CompilerParams(
            collective_id=0, has_side_effects=True, vmem_limit_bytes=60 * 1024 * 1024
        ),
    )(tokens, final_gain.reshape(NT, width), targets.reshape(2, 128), unembed)
    return loss.reshape(rows), grad


def solution(mesh):
    placed = (P(("dp", "pipe"), "tensor"), P(), P(("tensor", "pipe"), None), P("dp"))
    return jax.shard_map(
        body,
        mesh=mesh,
        in_specs=placed,
        out_specs=(P("dp"), P(("dp", "pipe"), "tensor")),
        check_vma=False,
    )
```

```python
import functools

import jax
import jax.numpy as jnp
from jax import lax
from jax.experimental import pallas as pl
from jax.experimental.pallas import tpu as pltpu
from jax.sharding import PartitionSpec as P

EPS = 1e-06
MESH = pl.DeviceIdType.MESH
NY, NC, NZ = 4, 2, 16
NT = NY * NC
BLK = 16
F32, BF16 = jnp.float32, jnp.bfloat16
NEAR = 4
NEAR_SLOTS = 2 * NEAR + 1
GROUPS = [[(4, 1)], [(2, 2), (5, 2)], [(0, 2), (7, 2)], [(9, 7)]]
FAR_OFFSETS = [8, 7, 9, 6, 10, 5, 11]
NEAR_OFFSETS = [4, 12, 3, 13, 2, 14, 1, 15]
Z_ORDER = FAR_OFFSETS + NEAR_OFFSETS
Y_ORDER = [2, 1, 3]


def slot_of(offset):
    return (offset + NEAR) % NZ


def kernel(
    tok_ref, gain_ref, tgt_ref, u_hbm, loss_ref, grad_ref,
    xs, us, ug, logits, q, term, send_t, send_o, core_t, core_o, y_t, y_o, own, z_send, z_recv,
    stat_send, stat_y, group, stat_z, twice, twice_int, u_sem, send_sem, recv_sem,
):
    dp = lax.axis_index("dp")
    t = lax.axis_index("tensor")
    z = lax.axis_index("pipe")
    y, c = t // NC, t % NC
    rows = BLK * NZ
    near_rows = NEAR_SLOTS * BLK
    width = tok_ref.shape[1]
    lanes = width // 128
    vocab = us.shape[1]
    count = [0]
    started = []

    def tensor_of(dy, dc):
        return lax.rem(y + dy, NY) * NC + lax.rem(c + dc, NC)

    def at_tensor(dy, dc):
        return (dp, tensor_of(dy, dc), z)

    def at_pipe(d):
        return (dp, t, lax.rem(z + d, NZ))

    def send(src, dst, device):
        i = count[0]
        count[0] += 1
        copy = pltpu.make_async_remote_copy(
            src_ref=src, dst_ref=dst, send_sem=send_sem.at[i], recv_sem=recv_sem.at[i],
            device_id=device, device_id_type=MESH,
        )
        copy.start()
        started.append(copy)
        return copy

    def slots(first, number=1):
        return pl.ds(first * BLK, number * BLK)

    def gain_of(k):
        return jnp.concatenate([gain_ref[pl.ds(lanes * k + i, 1), :] for i in range(lanes)], axis=1)

    barrier = pltpu.get_barrier_semaphore()
    for d in range(1, NZ):
        pl.semaphore_signal(barrier, inc=1, device_id=at_pipe(d), device_id_type=MESH)
    for j in range(1, NT):
        pl.semaphore_signal(barrier, inc=1, device_id=at_tensor(j // NC, j % NC), device_id_type=MESH)

    loads = []
    for k in range(NT):
        load = pltpu.make_async_copy(u_hbm.at[:, pl.ds(k * width, width)], us.at[k], u_sem.at[k])
        load.start()
        loads.append(load)
    own_copy = pltpu.make_async_copy(tok_ref, xs.at[t, slots(NEAR)], u_sem.at[NT])
    own_copy.start()

    for h in range(2):
        part = jnp.transpose(jnp.broadcast_to(tgt_ref[h : h + 1, :], (128, 128)))
        twice_int[pl.ds(h * 128, 128), :] = part
        twice_int[pl.ds(rows + h * 128, 128), :] = part
    first_block = lax.rem(z + NZ - NEAR, NZ)
    shift = pl.multiple_of(first_block * BLK, BLK)
    back = pl.multiple_of(rows - first_block * BLK, BLK)
    vocab_start = (t * NZ + z) * vocab
    own_copy.wait()
    pl.semaphore_wait(barrier, NZ - 1 + NT - 1)

    z_copies = {}
    for d in NEAR_OFFSETS:
        z_copies[slot_of(NZ - d)] = send(tok_ref, xs.at[t, slots(slot_of(NZ - d))], at_pipe(d))
    y_copies, core_copies = [], [[], [], [], []]

    def forward(g):
        for first, number in GROUPS[g]:
            piece = xs.at[t, slots(first, number)]
            for dy in Y_ORDER:
                y_copies.append((g, dy, first, number, send(piece, piece, at_tensor(dy, 0))))
            core_copies[g].append(send(piece, piece, at_tensor(0, 1)))

    def hand_over(g):
        for group_of, dy, first, number, copy in y_copies:
            if group_of == g:
                copy.wait_recv()
                piece = xs.at[tensor_of(NY - dy, 0), slots(first, number)]
                core_copies[g].append(send(piece, piece, at_tensor(0, 1)))

    def wait_group(g):
        for first, number in GROUPS[g]:
            for s in range(first, first + number):
                if s != 0 and s != NEAR_SLOTS - 1:
                    z_copies[s].wait_recv()

    forward(0)
    for k in range(NT):
        loads[k].wait()
    lane = lax.broadcasted_iota(jnp.int32, (rows, vocab), 1)
    local = twice_int[pl.ds(shift, rows), :] - vocab_start
    local = jnp.concatenate([local] * ((vocab + 127) // 128), axis=1)[:, :vocab]
    q[...] = (lane == local).astype(F32).astype(BF16)
    o_core, o_y = {}, {}
    for dy in Y_ORDER:
        k = tensor_of(dy, 1)
        send_o[k] = jnp.dot(q[...], us[k], preferred_element_type=F32).astype(BF16)
        o_core[dy] = send(send_o.at[k], core_o.at[dy], at_tensor(0, 1))
    wait_group(1)
    forward(1)
    z_copies[0].wait_recv()
    z_copies[NEAR_SLOTS - 1].wait_recv()
    far_ahead = xs.at[t, slots(0)]
    far_behind = xs.at[t, slots(NEAR_SLOTS - 1)]
    across = xs.at[t, pl.ds(pl.multiple_of(c * ((NEAR_SLOTS - 1) * BLK), BLK), BLK)]
    z_copies[slot_of(8)] = send(across, xs.at[t, slots(slot_of(8))], at_pipe(NEAR + c * (NZ - 2 * NEAR)))
    for j in (3, 2, 1):
        z_copies[NZ - j] = send(far_ahead, xs.at[t, slots(NZ - j)], at_pipe(j))
        z_copies[NEAR_SLOTS - 1 + j] = send(far_behind, xs.at[t, slots(NEAR_SLOTS - 1 + j)], at_pipe(NZ - j))
    wait_group(2)
    forward(2)
    hand_over(0)
    for dy in (0,):
        k = tensor_of(dy, 1)
        send_o[k] = jnp.dot(q[...], us[k], preferred_element_type=F32).astype(BF16)
        o_core[dy] = send(send_o.at[k], core_o.at[dy], at_tensor(0, 1))

    def sum_target(dy):
        k = tensor_of(dy, 0)
        mine = jnp.dot(q[...], us[k], preferred_element_type=F32)
        o_core[dy].wait_recv()
        send_o[k] = (mine + core_o[dy].astype(F32)).astype(BF16)

    def send_target(dy):
        k = tensor_of(dy, 0)
        o_y[dy] = send(send_o.at[k], y_o.at[dy - 1], at_tensor(dy, 0))

    sum_target(Y_ORDER[0])
    send_target(Y_ORDER[0])
    hand_over(1)

    def scale_u(k, _):
        ug[k] = (us[k].astype(F32) * gain_of(k)).astype(BF16)
        return 0

    lax.fori_loop(0, NT, scale_u, 0)
    wait_group(3)
    forward(3)
    hand_over(2)

    def products(first, size):
        part = pl.ds(first, size)
        logits[part, :] = jnp.zeros((size, vocab), F32)

        def multiply(k, total):
            x = xs[k, part, :]
            logits[part, :] += lax.dot_general(x, ug[k], (((1,), (1,)), ((), ())), preferred_element_type=F32)
            xf = x.astype(F32)
            xf = xf * xf
            for i in range(lanes):
                total = total + xf[:, i * 128 : (i + 1) * 128]
            return total

        squares = lax.fori_loop(0, NT, multiply, jnp.zeros((size, 128), F32))
        return lax.rsqrt(jnp.sum(squares, axis=1, keepdims=True) / (width * NT) + EPS)

    def softmax(first, size, inv):
        lane_id = lax.broadcasted_iota(jnp.int32, (size, 128), 1)
        column = lax.broadcasted_iota(jnp.int32, (size, vocab), 1)
        part = pl.ds(first, size)
        l = logits[part, :] * inv
        tgt = twice_int[pl.ds(pl.multiple_of(shift + first, BLK), size), :][:, :1] - vocab_start
        here = column == tgt
        top = jnp.max(l, axis=1, keepdims=True)
        e = jnp.where(here, 0.0, jnp.exp(l - top))
        q[part, :] = e.astype(BF16)
        total = jnp.sum(e, axis=1, keepdims=True)
        mixed = jnp.sum(e * l, axis=1, keepdims=True)
        picked = jnp.sum(jnp.where(here, l, 0.0), axis=1, keepdims=True)
        stats = jnp.where(lane_id == 0, top, jnp.where(lane_id == 1, total, jnp.where(lane_id == 2, mixed, picked)))
        twice[part, :] = stats
        twice[pl.ds(rows + first, size), :] = stats

    for dy in Y_ORDER[1:] + [0]:
        sum_target(dy)
    for g in range(3):
        for copy in core_copies[g]:
            copy.wait_recv()
    inv = products(0, near_rows)
    own_inv = inv[NEAR * BLK : (NEAR + 1) * BLK]
    for first in range(0, near_rows, 48):
        softmax(first, 48, inv[first : first + 48])
    hand_over(3)
    for dy in Y_ORDER[1:]:
        send_target(dy)
    for copy in core_copies[3]:
        copy.wait_recv()
    inv = products(near_rows, rows - near_rows)
    softmax(near_rows, 64, inv[:64])
    softmax(near_rows + 64, 48, inv[64:])
    for h in range(2):
        start = pl.multiple_of(back if h == 0 else lax.rem(back + 128, rows), BLK)
        turned = jnp.transpose(twice[pl.ds(start, 128), :])
        for i in range(4):
            stat_send[pl.ds(2 * i + h, 1), :] = turned[i : i + 1, :]
    y_stats = []
    for j in range(1, NT):
        y_stats.append(send(stat_send, stat_y.at[j], at_tensor(j // NC, j % NC)))

    t_core, t_y = {}, {}
    for dy in Y_ORDER + [0]:
        k = tensor_of(dy, 1)
        send_t[k] = jnp.dot(q[...], us[k], preferred_element_type=F32).astype(BF16)
        t_core[dy] = send(send_t.at[k], core_t.at[dy], at_tensor(0, 1))
    for dy in Y_ORDER + [0]:
        term[dy] = jnp.dot(q[...], us[tensor_of(dy, 0)], preferred_element_type=F32)

    def merge(tiles):
        top = tiles[0][0:2]
        for tile in tiles[1:]:
            top = jnp.maximum(top, tile[0:2])
        total = mixed = picked = jnp.zeros((2, 128), F32)
        for tile in tiles:
            factor = jnp.exp(tile[0:2] - top)
            total = total + factor * tile[2:4]
            mixed = mixed + factor * tile[4:6]
            picked = picked + tile[6:8]
        return top, total, mixed, picked

    def spread(value):
        for h in range(2):
            part = jnp.transpose(jnp.broadcast_to(value[h : h + 1, :], (128, 128)))
            twice[pl.ds(h * 128, 128), :] = part
            twice[pl.ds(rows + h * 128, 128), :] = part
        return twice[pl.ds(shift, rows), :]

    for copy in y_stats:
        copy.wait_recv()
    mine = stat_send[...]
    top, total, mixed, picked = merge([mine] + [stat_y[j] for j in range(1, NT)])
    group[0:2, :] = top
    group[2:4, :] = total
    group[4:6, :] = mixed
    group[6:8, :] = picked
    z_stats = []
    for d in Z_ORDER:
        z_stats.append(send(group, stat_z.at[d], at_pipe(d)))
    own[0] = spread(jnp.exp(mine[0:2] - top))
    own[1] = spread(jnp.exp(stat_y[1][0:2] - top))
    far, near = (near_rows, rows - near_rows), (0, near_rows)

    def add_core(dy, first, size):
        part = pl.ds(first, size)
        own_factor = jnp.concatenate([own[0, part, :]] * lanes, axis=1)
        core_factor = jnp.concatenate([own[1, part, :]] * lanes, axis=1)
        return term[dy, part, :] * own_factor + core_t[dy, part, :].astype(F32) * core_factor

    for first, size in (far, near):
        part = pl.ds(first, size)
        for dy in Y_ORDER:
            if first:
                t_core[dy].wait_recv()
            k = tensor_of(dy, 0)
            send_t[k, part, :] = add_core(dy, first, size).astype(BF16)
            t_y[dy, first] = send(send_t.at[k, part], y_t.at[dy - 1, part], at_tensor(dy, 0))
    t_core[0].wait_recv()
    for dy in Y_ORDER:
        o_y[dy].wait_recv()
    for first, size in (far, near):
        part = pl.ds(first, size)
        target = send_o[t, part, :].astype(F32)
        for dy in range(NY - 1):
            target = target + y_o[dy, part, :].astype(F32)
        term[1, part, :] = target
        term[0, part, :] = add_core(0, first, size)
    for copy in z_stats:
        copy.wait_recv()
    group_top = group[0:2]
    top, total, mixed, picked = merge([group[...]] + [stat_z[d] for d in range(1, NZ)])
    full = total + jnp.exp(picked - top)
    loss_ref[...] = top + jnp.log(full) - picked
    own[0] = spread(jnp.exp(group_top - top) / full)
    own[1] = spread(total / full)
    own_dot = spread((mixed - total * picked) / full)[NEAR * BLK : (NEAR + 1) * BLK]
    z_grads = {}
    for (first, size), offsets in ((far, FAR_OFFSETS), (near, NEAR_OFFSETS)):
        part = pl.ds(first, size)
        for dy in Y_ORDER:
            t_y[dy, first].wait_recv()
        value = term[0, part, :]
        for dy in range(NY - 1):
            value = value + y_t[dy, part, :].astype(F32)
        scale = jnp.concatenate([own[0, part, :]] * lanes, axis=1)
        drop = jnp.concatenate([own[1, part, :]] * lanes, axis=1)
        value = value * scale - term[1, part, :] * drop
        z_send[part, :] = value.astype(BF16)
        if first == 0:
            term[2, slots(NEAR), :] = value[NEAR * BLK : (NEAR + 1) * BLK]
        for d in offsets:
            z_grads[d] = send(z_send.at[slots(slot_of(d))], z_recv.at[d], at_pipe(d))
    grad = term[2, slots(NEAR), :]
    for d in reversed(Z_ORDER):
        z_grads[d].wait_recv()
        grad = grad + z_recv[d].astype(F32)
    stream = tok_ref[...].astype(F32)
    weighted = grad * gain_of(t)
    dots = own_dot[:, :1] / (own_inv * (width * NT))
    grad_ref[...] = own_inv * (weighted - stream * (own_inv * own_inv * dots))
    for copy in started:
        copy.wait_send()


def body(tokens, final_gain, unembed, targets):
    vocab, features = unembed.shape
    width = tokens.shape[1]
    rows = targets.shape[0]
    vmem = pl.BlockSpec(memory_space=pltpu.VMEM)
    loss, grad = pl.pallas_call(
        kernel,
        out_shape=(
            jax.ShapeDtypeStruct((2, 128), F32),
            jax.ShapeDtypeStruct(tokens.shape, F32),
        ),
        in_specs=[vmem, vmem, vmem, pl.BlockSpec(memory_space=pl.ANY)],
        out_specs=(vmem, vmem),
        scratch_shapes=[
            pltpu.VMEM((NT, rows, width), BF16),
            pltpu.VMEM((NT, vocab, width), BF16),
            pltpu.VMEM((NT, vocab, width), BF16),
            pltpu.VMEM((rows, vocab), F32),
            pltpu.VMEM((rows, vocab), BF16),
            pltpu.VMEM((NY, rows, width), F32),
            pltpu.VMEM((NT, rows, width), BF16),
            pltpu.VMEM((NT, rows, width), BF16),
            pltpu.VMEM((NY, rows, width), BF16),
            pltpu.VMEM((NY, rows, width), BF16),
            pltpu.VMEM((NY - 1, rows, width), BF16),
            pltpu.VMEM((NY - 1, rows, width), BF16),
            pltpu.VMEM((2, rows, 128), F32),
            pltpu.VMEM((rows, width), BF16),
            pltpu.VMEM((NZ, BLK, width), BF16),
            pltpu.VMEM((8, 128), F32),
            pltpu.VMEM((NT, 8, 128), F32),
            pltpu.VMEM((8, 128), F32),
            pltpu.VMEM((NZ, 8, 128), F32),
            pltpu.VMEM((2 * rows, 128), F32),
            pltpu.VMEM((2 * rows, 128), jnp.int32),
            pltpu.SemaphoreType.DMA((NT + 1,)),
            pltpu.SemaphoreType.DMA((160,)),
            pltpu.SemaphoreType.DMA((160,)),
        ],
        compiler_params=pltpu.CompilerParams(
            collective_id=0, has_side_effects=True, vmem_limit_bytes=60 * 1024 * 1024
        ),
    )(tokens, final_gain.reshape(features // 128, 128), targets.reshape(2, 128), unembed)
    return loss.reshape(rows), grad


def solution(mesh):
    placed = (P(("dp", "pipe"), "tensor"), P(), P(("tensor", "pipe"), None), P("dp"))
    return jax.shard_map(
        body,
        mesh=mesh,
        in_specs=placed,
        out_specs=(P("dp"), P(("dp", "pipe"), "tensor")),
        check_vma=False,
    )
```

```python
import functools

import jax
import jax.numpy as jnp
from jax import lax
from jax.experimental import pallas as pl
from jax.experimental.pallas import tpu as pltpu
from jax.sharding import PartitionSpec as P

EPS = 1e-06
MESH = pl.DeviceIdType.MESH
NY, NC, NZ = 4, 2, 16
NT = NY * NC
BLK = 16
F32, BF16 = jnp.float32, jnp.bfloat16
NEAR = 4
NEAR_SLOTS = 2 * NEAR + 1
GROUPS = [[(4, 1)], [(2, 2), (5, 2)], [(0, 2), (7, 2)], [(9, 2), (14, 2)], [(11, 3)]]
FAR_OFFSETS = [8, 7, 9, 6, 10, 5, 11]
NEAR_OFFSETS = [4, 12, 3, 13, 2, 14, 1, 15]
Z_ORDER = FAR_OFFSETS + NEAR_OFFSETS
Y_ORDER = [2, 1, 3]
SUMS = [([(9, 7)], FAR_OFFSETS), ([(0, 3), (6, 3)], NEAR_OFFSETS[:6]), ([(3, 3)], NEAR_OFFSETS[6:])]


def slot_of(offset):
    return (offset + NEAR) % NZ


def kernel(
    tok_ref, gain_ref, tgt_ref, u_hbm, loss_ref, grad_ref,
    xs, us, ug, logits, q, term, send_t, send_o, core_t, core_o, y_t, y_o, own, z_send, z_recv,
    stat_send, stat_y, group, stat_z, twice, twice_int, u_sem, send_sem, recv_sem,
):
    dp = lax.axis_index("dp")
    t = lax.axis_index("tensor")
    z = lax.axis_index("pipe")
    y, c = t // NC, t % NC
    rows = BLK * NZ
    near_rows = NEAR_SLOTS * BLK
    width = tok_ref.shape[1]
    lanes = width // 128
    vocab = us.shape[1]
    count = [0]
    started = []

    def tensor_of(dy, dc):
        return lax.rem(y + dy, NY) * NC + lax.rem(c + dc, NC)

    def at_tensor(dy, dc):
        return (dp, tensor_of(dy, dc), z)

    def at_pipe(d):
        return (dp, t, lax.rem(z + d, NZ))

    def send(src, dst, device):
        i = count[0]
        count[0] += 1
        copy = pltpu.make_async_remote_copy(
            src_ref=src, dst_ref=dst, send_sem=send_sem.at[i], recv_sem=recv_sem.at[i],
            device_id=device, device_id_type=MESH,
        )
        copy.start()
        started.append(copy)
        return copy

    def slots(first, number=1):
        return pl.ds(first * BLK, number * BLK)

    def gain_of(k):
        return jnp.concatenate([gain_ref[pl.ds(lanes * k + i, 1), :] for i in range(lanes)], axis=1)

    barrier = pltpu.get_barrier_semaphore()
    for d in range(1, NZ):
        pl.semaphore_signal(barrier, inc=1, device_id=at_pipe(d), device_id_type=MESH)
    for j in range(1, NT):
        pl.semaphore_signal(barrier, inc=1, device_id=at_tensor(j // NC, j % NC), device_id_type=MESH)

    loads = []
    for k in range(NT):
        load = pltpu.make_async_copy(u_hbm.at[:, pl.ds(k * width, width)], us.at[k], u_sem.at[k])
        load.start()
        loads.append(load)
    own_copy = pltpu.make_async_copy(tok_ref, xs.at[t, slots(NEAR)], u_sem.at[NT])
    own_copy.start()

    for h in range(2):
        part = jnp.transpose(jnp.broadcast_to(tgt_ref[h : h + 1, :], (128, 128)))
        twice_int[pl.ds(h * 128, 128), :] = part
        twice_int[pl.ds(rows + h * 128, 128), :] = part
    first_block = lax.rem(z + NZ - NEAR, NZ)
    shift = pl.multiple_of(first_block * BLK, BLK)
    back = pl.multiple_of(rows - first_block * BLK, BLK)
    vocab_start = (t * NZ + z) * vocab
    own_copy.wait()
    pl.semaphore_wait(barrier, NZ - 1 + NT - 1)

    z_copies = {}
    for d in NEAR_OFFSETS:
        z_copies[slot_of(NZ - d)] = send(tok_ref, xs.at[t, slots(slot_of(NZ - d))], at_pipe(d))
    y_copies, core_copies = [], [[] for _ in GROUPS]

    def forward(g):
        for first, number in GROUPS[g]:
            piece = xs.at[t, slots(first, number)]
            for dy in Y_ORDER:
                y_copies.append((g, dy, first, number, send(piece, piece, at_tensor(dy, 0))))
            core_copies[g].append(send(piece, piece, at_tensor(0, 1)))

    def hand_over(g):
        for group_of, dy, first, number, copy in y_copies:
            if group_of == g:
                copy.wait_recv()
                piece = xs.at[tensor_of(NY - dy, 0), slots(first, number)]
                core_copies[g].append(send(piece, piece, at_tensor(0, 1)))

    def wait_group(g):
        for first, number in GROUPS[g]:
            for s in range(first, first + number):
                if s != 0 and s != NEAR_SLOTS - 1:
                    z_copies[s].wait_recv()

    forward(0)
    for k in range(NT):
        loads[k].wait()
    lane = lax.broadcasted_iota(jnp.int32, (rows, vocab), 1)
    local = twice_int[pl.ds(shift, rows), :] - vocab_start
    local = jnp.concatenate([local] * ((vocab + 127) // 128), axis=1)[:, :vocab]
    q[...] = (lane == local).astype(F32).astype(BF16)
    o_core, o_y = {}, {}
    for dy in Y_ORDER:
        k = tensor_of(dy, 1)
        send_o[k] = jnp.dot(q[...], us[k], preferred_element_type=F32).astype(BF16)
        o_core[dy] = send(send_o.at[k], core_o.at[dy], at_tensor(0, 1))
    wait_group(1)
    forward(1)
    z_copies[0].wait_recv()
    z_copies[NEAR_SLOTS - 1].wait_recv()
    far_ahead = xs.at[t, slots(0)]
    far_behind = xs.at[t, slots(NEAR_SLOTS - 1)]
    across = xs.at[t, pl.ds(pl.multiple_of(c * ((NEAR_SLOTS - 1) * BLK), BLK), BLK)]
    z_copies[slot_of(8)] = send(across, xs.at[t, slots(slot_of(8))], at_pipe(NEAR + c * (NZ - 2 * NEAR)))
    for j in (1, 2, 3):
        z_copies[NZ - j] = send(far_ahead, xs.at[t, slots(NZ - j)], at_pipe(j))
        z_copies[NEAR_SLOTS - 1 + j] = send(far_behind, xs.at[t, slots(NEAR_SLOTS - 1 + j)], at_pipe(NZ - j))
    wait_group(2)
    forward(2)
    hand_over(0)
    for dy in (0,):
        k = tensor_of(dy, 1)
        send_o[k] = jnp.dot(q[...], us[k], preferred_element_type=F32).astype(BF16)
        o_core[dy] = send(send_o.at[k], core_o.at[dy], at_tensor(0, 1))

    def sum_target(dy):
        k = tensor_of(dy, 0)
        mine = jnp.dot(q[...], us[k], preferred_element_type=F32)
        o_core[dy].wait_recv()
        send_o[k] = (mine + core_o[dy].astype(F32)).astype(BF16)

    def send_target(dy):
        k = tensor_of(dy, 0)
        o_y[dy] = send(send_o.at[k], y_o.at[dy - 1], at_tensor(dy, 0))

    sum_target(Y_ORDER[0])
    send_target(Y_ORDER[0])
    hand_over(1)

    def scale_u(k, _):
        ug[k] = (us[k].astype(F32) * gain_of(k)).astype(BF16)
        return 0

    lax.fori_loop(0, NT, scale_u, 0)
    wait_group(3)
    forward(3)
    wait_group(4)
    forward(4)
    hand_over(2)

    def products(first, size):
        part = pl.ds(first, size)
        logits[part, :] = jnp.zeros((size, vocab), F32)

        def multiply(k, total):
            x = xs[k, part, :]
            logits[part, :] += lax.dot_general(x, ug[k], (((1,), (1,)), ((), ())), preferred_element_type=F32)
            xf = x.astype(F32)
            xf = xf * xf
            for i in range(lanes):
                total = total + xf[:, i * 128 : (i + 1) * 128]
            return total

        squares = lax.fori_loop(0, NT, multiply, jnp.zeros((size, 128), F32))
        return lax.rsqrt(jnp.sum(squares, axis=1, keepdims=True) / (width * NT) + EPS)

    def softmax(first, size, inv):
        lane_id = lax.broadcasted_iota(jnp.int32, (size, 128), 1)
        column = lax.broadcasted_iota(jnp.int32, (size, vocab), 1)
        part = pl.ds(first, size)
        l = logits[part, :] * inv
        tgt = twice_int[pl.ds(pl.multiple_of(shift + first, BLK), size), :][:, :1] - vocab_start
        here = column == tgt
        top = jnp.max(l, axis=1, keepdims=True)
        e = jnp.where(here, 0.0, jnp.exp(l - top))
        q[part, :] = e.astype(BF16)
        total = jnp.sum(e, axis=1, keepdims=True)
        mixed = jnp.sum(e * l, axis=1, keepdims=True)
        picked = jnp.sum(jnp.where(here, l, 0.0), axis=1, keepdims=True)
        stats = jnp.where(lane_id == 0, top, jnp.where(lane_id == 1, total, jnp.where(lane_id == 2, mixed, picked)))
        twice[part, :] = stats
        twice[pl.ds(rows + first, size), :] = stats

    for dy in Y_ORDER[1:] + [0]:
        sum_target(dy)
    for g in range(3):
        for copy in core_copies[g]:
            copy.wait_recv()
    inv = products(0, near_rows)
    own_inv = inv[NEAR * BLK : (NEAR + 1) * BLK]
    for first in range(0, near_rows, 48):
        softmax(first, 48, inv[first : first + 48])
    hand_over(3)
    hand_over(4)
    for dy in Y_ORDER[1:]:
        send_target(dy)
    for copy in core_copies[3] + core_copies[4]:
        copy.wait_recv()
    inv = products(near_rows, rows - near_rows)
    softmax(near_rows, 64, inv[:64])
    softmax(near_rows + 64, 48, inv[64:])
    for h in range(2):
        start = pl.multiple_of(back if h == 0 else lax.rem(back + 128, rows), BLK)
        turned = jnp.transpose(twice[pl.ds(start, 128), :])
        for i in range(4):
            stat_send[pl.ds(2 * i + h, 1), :] = turned[i : i + 1, :]
    y_stats = []
    for j in range(1, NT):
        y_stats.append(send(stat_send, stat_y.at[j], at_tensor(j // NC, j % NC)))

    t_core, t_y = {}, {}
    for dy in Y_ORDER + [0]:
        k = tensor_of(dy, 1)
        send_t[k] = jnp.dot(q[...], us[k], preferred_element_type=F32).astype(BF16)
        t_core[dy] = send(send_t.at[k], core_t.at[dy], at_tensor(0, 1))
    for dy in Y_ORDER + [0]:
        term[dy] = jnp.dot(q[...], us[tensor_of(dy, 0)], preferred_element_type=F32)

    def merge(tiles):
        top = tiles[0][0:2]
        for tile in tiles[1:]:
            top = jnp.maximum(top, tile[0:2])
        total = mixed = picked = jnp.zeros((2, 128), F32)
        for tile in tiles:
            factor = jnp.exp(tile[0:2] - top)
            total = total + factor * tile[2:4]
            mixed = mixed + factor * tile[4:6]
            picked = picked + tile[6:8]
        return top, total, mixed, picked

    def spread(value):
        for h in range(2):
            part = jnp.transpose(jnp.broadcast_to(value[h : h + 1, :], (128, 128)))
            twice[pl.ds(h * 128, 128), :] = part
            twice[pl.ds(rows + h * 128, 128), :] = part
        return twice[pl.ds(shift, rows), :]

    for copy in y_stats:
        copy.wait_recv()
    mine = stat_send[...]
    top, total, mixed, picked = merge([mine] + [stat_y[j] for j in range(1, NT)])
    group[0:2, :] = top
    group[2:4, :] = total
    group[4:6, :] = mixed
    group[6:8, :] = picked
    own[0] = spread(jnp.exp(mine[0:2] - top))
    own[1] = spread(jnp.exp(stat_y[1][0:2] - top))

    def add_core(dy, part):
        own_factor = jnp.concatenate([own[0, part, :]] * lanes, axis=1)
        core_factor = jnp.concatenate([own[1, part, :]] * lanes, axis=1)
        return term[dy, part, :] * own_factor + core_t[dy, part, :].astype(F32) * core_factor

    z_stats = []
    for pieces, _ in SUMS:
        for dy in Y_ORDER:
            if not z_stats:
                t_core[dy].wait_recv()
            k = tensor_of(dy, 0)
            for first, number in pieces:
                part = slots(first, number)
                send_t[k, part, :] = add_core(dy, part).astype(BF16)
                t_y[dy, first] = send(send_t.at[k, part], y_t.at[dy - 1, part], at_tensor(dy, 0))
        if not z_stats:
            for d in Z_ORDER:
                z_stats.append(send(group, stat_z.at[d], at_pipe(d)))
    t_core[0].wait_recv()
    for dy in Y_ORDER:
        o_y[dy].wait_recv()
    for pieces, _ in SUMS:
        for first, number in pieces:
            part = slots(first, number)
            target = send_o[t, part, :].astype(F32)
            for dy in range(NY - 1):
                target = target + y_o[dy, part, :].astype(F32)
            term[1, part, :] = target
            term[0, part, :] = add_core(0, part)
    for copy in z_stats:
        copy.wait_recv()
    group_top = group[0:2]
    top, total, mixed, picked = merge([group[...]] + [stat_z[d] for d in range(1, NZ)])
    full = total + jnp.exp(picked - top)
    loss_ref[...] = top + jnp.log(full) - picked
    own[0] = spread(jnp.exp(group_top - top) / full)
    own[1] = spread(total / full)
    own_dot = spread((mixed - total * picked) / full)[NEAR * BLK : (NEAR + 1) * BLK]
    z_grads = {}
    for pieces, offsets in SUMS:
        for first, number in pieces:
            part = slots(first, number)
            for dy in Y_ORDER:
                t_y[dy, first].wait_recv()
            value = term[0, part, :]
            for dy in range(NY - 1):
                value = value + y_t[dy, part, :].astype(F32)
            scale = jnp.concatenate([own[0, part, :]] * lanes, axis=1)
            drop = jnp.concatenate([own[1, part, :]] * lanes, axis=1)
            value = value * scale - term[1, part, :] * drop
            z_send[part, :] = value.astype(BF16)
            if first <= NEAR < first + number:
                term[2, slots(NEAR), :] = value[(NEAR - first) * BLK : (NEAR - first + 1) * BLK]
        for d in offsets:
            z_grads[d] = send(z_send.at[slots(slot_of(d))], z_recv.at[d], at_pipe(d))
    grad = term[2, slots(NEAR), :]
    for d in Z_ORDER:
        z_grads[d].wait_recv()
        grad = grad + z_recv[d].astype(F32)
    stream = tok_ref[...].astype(F32)
    weighted = grad * gain_of(t)
    dots = own_dot[:, :1] / (own_inv * (width * NT))
    grad_ref[...] = own_inv * (weighted - stream * (own_inv * own_inv * dots))
    for copy in started:
        copy.wait_send()


def hand_out(loss_ref, grad_ref, loss_out, grad_out):
    loss_out[...] = loss_ref[...]
    grad_out[...] = grad_ref[...]


def body(tokens, final_gain, unembed, targets):
    vocab, features = unembed.shape
    width = tokens.shape[1]
    rows = targets.shape[0]
    vmem = pl.BlockSpec(memory_space=pltpu.VMEM)
    results = (
        jax.ShapeDtypeStruct((2, 128), F32),
        jax.ShapeDtypeStruct(tokens.shape, F32),
    )
    loss, grad = pl.pallas_call(
        kernel,
        out_shape=results,
        in_specs=[vmem, vmem, vmem, pl.BlockSpec(memory_space=pl.ANY)],
        out_specs=(vmem, vmem),
        scratch_shapes=[
            pltpu.VMEM((NT, rows, width), BF16),
            pltpu.VMEM((NT, vocab, width), BF16),
            pltpu.VMEM((NT, vocab, width), BF16),
            pltpu.VMEM((rows, vocab), F32),
            pltpu.VMEM((rows, vocab), BF16),
            pltpu.VMEM((NY, rows, width), F32),
            pltpu.VMEM((NT, rows, width), BF16),
            pltpu.VMEM((NT, rows, width), BF16),
            pltpu.VMEM((NY, rows, width), BF16),
            pltpu.VMEM((NY, rows, width), BF16),
            pltpu.VMEM((NY - 1, rows, width), BF16),
            pltpu.VMEM((NY - 1, rows, width), BF16),
            pltpu.VMEM((2, rows, 128), F32),
            pltpu.VMEM((rows, width), BF16),
            pltpu.VMEM((NZ, BLK, width), BF16),
            pltpu.VMEM((8, 128), F32),
            pltpu.VMEM((NT, 8, 128), F32),
            pltpu.VMEM((8, 128), F32),
            pltpu.VMEM((NZ, 8, 128), F32),
            pltpu.VMEM((2 * rows, 128), F32),
            pltpu.VMEM((2 * rows, 128), jnp.int32),
            pltpu.SemaphoreType.DMA((NT + 1,)),
            pltpu.SemaphoreType.DMA((160,)),
            pltpu.SemaphoreType.DMA((160,)),
        ],
        compiler_params=pltpu.CompilerParams(
            collective_id=0, has_side_effects=True, vmem_limit_bytes=60 * 1024 * 1024
        ),
    )(tokens, final_gain.reshape(features // 128, 128), targets.reshape(2, 128), unembed)
    loss, grad = pl.pallas_call(
        hand_out, out_shape=results, in_specs=[vmem, vmem], out_specs=(vmem, vmem)
    )(loss, grad)
    return loss.reshape(rows), grad


def solution(mesh):
    placed = (P(("dp", "pipe"), "tensor"), P(), P(("tensor", "pipe"), None), P("dp"))
    return jax.shard_map(
        body,
        mesh=mesh,
        in_specs=placed,
        out_specs=(P("dp"), P(("dp", "pipe"), "tensor")),
        check_vma=False,
    )
```

```python
import functools

import jax
import jax.numpy as jnp
from jax import lax
from jax.experimental import pallas as pl
from jax.experimental.pallas import tpu as pltpu
from jax.sharding import PartitionSpec as P

EPS = 1e-06
MESH = pl.DeviceIdType.MESH
NY, NC, NZ = 4, 2, 16
NT = NY * NC
BLK = 16
F32, BF16 = jnp.float32, jnp.bfloat16
NEAR = 4
NEAR_SLOTS = 2 * NEAR + 1
GROUPS = [[(4, 1)], [(2, 2), (5, 2)], [(0, 2), (7, 2)], [(9, 2), (14, 2)], [(11, 3)]]
FAR_OFFSETS = [8, 7, 9, 6, 10, 5, 11]
NEAR_OFFSETS = [4, 12, 3, 13, 2, 14, 1, 15]
Z_ORDER = FAR_OFFSETS + NEAR_OFFSETS
Y_ORDER = [2, 1, 3]
SUMS = [([(11, 3)], FAR_OFFSETS[:3]), ([(9, 2), (14, 2)], FAR_OFFSETS[3:]), ([(0, 3), (6, 3)], NEAR_OFFSETS[:6]), ([(3, 3)], NEAR_OFFSETS[6:])]


def slot_of(offset):
    return (offset + NEAR) % NZ


def kernel(
    tok_ref, gain_ref, tgt_ref, u_hbm, loss_ref, grad_ref,
    xs, us, ug, logits, q, term, send_t, send_o, core_t, core_o, y_t, y_o, o_half, own, z_send, z_recv,
    stat_send, stat_y, group, stat_z, twice, twice_int, u_sem, send_sem, recv_sem,
):
    dp = lax.axis_index("dp")
    t = lax.axis_index("tensor")
    z = lax.axis_index("pipe")
    y, c = t // NC, t % NC
    rows = BLK * NZ
    near_rows = NEAR_SLOTS * BLK
    width = tok_ref.shape[1]
    lanes = width // 128
    vocab = us.shape[1]
    count = [0]
    started = []

    def tensor_of(dy, dc):
        return lax.rem(y + dy, NY) * NC + lax.rem(c + dc, NC)

    def at_tensor(dy, dc):
        return (dp, tensor_of(dy, dc), z)

    def at_pipe(d):
        return (dp, t, lax.rem(z + d, NZ))

    def send(src, dst, device):
        i = count[0]
        count[0] += 1
        copy = pltpu.make_async_remote_copy(
            src_ref=src, dst_ref=dst, send_sem=send_sem.at[i], recv_sem=recv_sem.at[i],
            device_id=device, device_id_type=MESH,
        )
        copy.start()
        started.append(copy)
        return copy

    def slots(first, number=1):
        return pl.ds(first * BLK, number * BLK)

    def gain_of(k):
        return jnp.concatenate([gain_ref[pl.ds(lanes * k + i, 1), :] for i in range(lanes)], axis=1)

    barrier = pltpu.get_barrier_semaphore()
    for d in range(1, NZ):
        pl.semaphore_signal(barrier, inc=1, device_id=at_pipe(d), device_id_type=MESH)
    for j in range(1, NT):
        pl.semaphore_signal(barrier, inc=1, device_id=at_tensor(j // NC, j % NC), device_id_type=MESH)

    loads = []
    for k in range(NT):
        load = pltpu.make_async_copy(u_hbm.at[:, pl.ds(k * width, width)], us.at[k], u_sem.at[k])
        load.start()
        loads.append(load)
    own_copy = pltpu.make_async_copy(tok_ref, xs.at[t, slots(NEAR)], u_sem.at[NT])
    own_copy.start()

    for h in range(2):
        part = jnp.transpose(jnp.broadcast_to(tgt_ref[h : h + 1, :], (128, 128)))
        twice_int[pl.ds(h * 128, 128), :] = part
        twice_int[pl.ds(rows + h * 128, 128), :] = part
    first_block = lax.rem(z + NZ - NEAR, NZ)
    shift = pl.multiple_of(first_block * BLK, BLK)
    back = pl.multiple_of(rows - first_block * BLK, BLK)
    vocab_start = (t * NZ + z) * vocab
    own_copy.wait()
    pl.semaphore_wait(barrier, NZ - 1 + NT - 1)

    z_copies = {}
    for d in NEAR_OFFSETS:
        z_copies[slot_of(NZ - d)] = send(tok_ref, xs.at[t, slots(slot_of(NZ - d))], at_pipe(d))
    y_copies, core_copies = [], [[] for _ in GROUPS]

    def forward(g):
        for first, number in GROUPS[g]:
            piece = xs.at[t, slots(first, number)]
            for dy in Y_ORDER:
                y_copies.append((g, dy, first, number, send(piece, piece, at_tensor(dy, 0))))
            core_copies[g].append(send(piece, piece, at_tensor(0, 1)))

    def hand_over(g):
        for group_of, dy, first, number, copy in y_copies:
            if group_of == g:
                copy.wait_recv()
                piece = xs.at[tensor_of(NY - dy, 0), slots(first, number)]
                core_copies[g].append(send(piece, piece, at_tensor(0, 1)))

    def wait_group(g):
        for first, number in GROUPS[g]:
            for s in range(first, first + number):
                if s != 0 and s != NEAR_SLOTS - 1:
                    z_copies[s].wait_recv()

    forward(0)
    for k in range(NT):
        loads[k].wait()
    lane = lax.broadcasted_iota(jnp.int32, (rows, vocab), 1)
    local = twice_int[pl.ds(shift, rows), :] - vocab_start
    local = jnp.concatenate([local] * ((vocab + 127) // 128), axis=1)[:, :vocab]
    q[...] = (lane == local).astype(F32).astype(BF16)
    o_core, o_y = {}, {}
    for dy in Y_ORDER:
        k = tensor_of(dy, 1)
        send_o[k] = jnp.dot(q[...], us[k], preferred_element_type=F32).astype(BF16)
        o_core[dy] = send(send_o.at[k], core_o.at[dy], at_tensor(0, 1))
    wait_group(1)
    forward(1)
    z_copies[0].wait_recv()
    z_copies[NEAR_SLOTS - 1].wait_recv()
    far_ahead = xs.at[t, slots(0)]
    far_behind = xs.at[t, slots(NEAR_SLOTS - 1)]
    across = xs.at[t, pl.ds(pl.multiple_of(c * ((NEAR_SLOTS - 1) * BLK), BLK), BLK)]
    z_copies[slot_of(8)] = send(across, xs.at[t, slots(slot_of(8))], at_pipe(NEAR + c * (NZ - 2 * NEAR)))
    for j in (1, 2, 3):
        z_copies[NZ - j] = send(far_ahead, xs.at[t, slots(NZ - j)], at_pipe(j))
        z_copies[NEAR_SLOTS - 1 + j] = send(far_behind, xs.at[t, slots(NEAR_SLOTS - 1 + j)], at_pipe(NZ - j))
    wait_group(2)
    forward(2)
    hand_over(0)
    for dy in (0,):
        k = tensor_of(dy, 1)
        send_o[k] = jnp.dot(q[...], us[k], preferred_element_type=F32).astype(BF16)
        o_core[dy] = send(send_o.at[k], core_o.at[dy], at_tensor(0, 1))

    half = width // 2
    cuts = {1: pl.ds(0, half), 3: pl.ds(half, half)}
    o_through = {}

    def sum_target(dy):
        k = tensor_of(dy, 0)
        total = jnp.dot(q[...], us[k], preferred_element_type=F32)
        o_core[dy].wait_recv()
        send_o[k] = (total + core_o[dy].astype(F32)).astype(BF16)
        if dy in cuts:
            o_through[dy].wait_recv()
            passing = o_half[dy // 2].astype(F32)
            send_o[k, :, cuts[dy]] = (send_o[k, :, cuts[dy]].astype(F32) + passing).astype(BF16)

    def send_target(dy):
        o_y[dy] = send(send_o.at[tensor_of(dy, 0)], y_o.at[dy // 2], at_tensor(dy, 0))

    sum_target(2)
    for dy in cuts:
        o_through[dy] = send(send_o.at[tensor_of(2, 0), :, cuts[dy]], o_half.at[dy // 2], at_tensor(dy, 0))
    hand_over(1)

    def scale_u(k, _):
        ug[k] = (us[k].astype(F32) * gain_of(k)).astype(BF16)
        return 0

    lax.fori_loop(0, NT, scale_u, 0)
    wait_group(3)
    forward(3)
    wait_group(4)
    forward(4)
    hand_over(2)

    def products(first, size):
        part = pl.ds(first, size)
        logits[part, :] = jnp.zeros((size, vocab), F32)

        def multiply(k, total):
            x = xs[k, part, :]
            logits[part, :] += lax.dot_general(x, ug[k], (((1,), (1,)), ((), ())), preferred_element_type=F32)
            xf = x.astype(F32)
            xf = xf * xf
            for i in range(lanes):
                total = total + xf[:, i * 128 : (i + 1) * 128]
            return total

        squares = lax.fori_loop(0, NT, multiply, jnp.zeros((size, 128), F32))
        return lax.rsqrt(jnp.sum(squares, axis=1, keepdims=True) / (width * NT) + EPS)

    def softmax(first, size, inv):
        lane_id = lax.broadcasted_iota(jnp.int32, (size, 128), 1)
        column = lax.broadcasted_iota(jnp.int32, (size, vocab), 1)
        part = pl.ds(first, size)
        l = logits[part, :] * inv
        tgt = twice_int[pl.ds(pl.multiple_of(shift + first, BLK), size), :][:, :1] - vocab_start
        here = column == tgt
        top = jnp.max(l, axis=1, keepdims=True)
        e = jnp.where(here, 0.0, jnp.exp(l - top))
        q[part, :] = e.astype(BF16)
        total = jnp.sum(e, axis=1, keepdims=True)
        mixed = jnp.sum(e * l, axis=1, keepdims=True)
        picked = jnp.sum(jnp.where(here, l, 0.0), axis=1, keepdims=True)
        stats = jnp.where(lane_id == 0, top, jnp.where(lane_id == 1, total, jnp.where(lane_id == 2, mixed, picked)))
        twice[part, :] = stats
        twice[pl.ds(rows + first, size), :] = stats

    for dy in Y_ORDER[1:] + [0]:
        sum_target(dy)
    for g in range(3):
        for copy in core_copies[g]:
            copy.wait_recv()
    inv = products(0, near_rows)
    own_inv = inv[NEAR * BLK : (NEAR + 1) * BLK]
    for first in range(0, near_rows, 48):
        softmax(first, 48, inv[first : first + 48])
    hand_over(3)
    hand_over(4)
    for dy in cuts:
        send_target(dy)
    for copy in core_copies[3] + core_copies[4]:
        copy.wait_recv()
    inv = products(near_rows, rows - near_rows)
    softmax(near_rows, 64, inv[:64])
    softmax(near_rows + 64, 48, inv[64:])
    for h in range(2):
        start = pl.multiple_of(back if h == 0 else lax.rem(back + 128, rows), BLK)
        turned = jnp.transpose(twice[pl.ds(start, 128), :])
        for i in range(4):
            stat_send[pl.ds(2 * i + h, 1), :] = turned[i : i + 1, :]
    y_stats = []
    for j in range(1, NT):
        y_stats.append(send(stat_send, stat_y.at[j], at_tensor(j // NC, j % NC)))

    t_core, t_y = {}, {}
    for dy in Y_ORDER + [0]:
        k = tensor_of(dy, 1)
        send_t[k] = jnp.dot(q[...], us[k], preferred_element_type=F32).astype(BF16)
        t_core[dy] = send(send_t.at[k], core_t.at[dy], at_tensor(0, 1))
    for dy in Y_ORDER + [0]:
        term[dy] = jnp.dot(q[...], us[tensor_of(dy, 0)], preferred_element_type=F32)

    def merge(tiles):
        top = tiles[0][0:2]
        for tile in tiles[1:]:
            top = jnp.maximum(top, tile[0:2])
        total = mixed = picked = jnp.zeros((2, 128), F32)
        for tile in tiles:
            factor = jnp.exp(tile[0:2] - top)
            total = total + factor * tile[2:4]
            mixed = mixed + factor * tile[4:6]
            picked = picked + tile[6:8]
        return top, total, mixed, picked

    def spread(value):
        for h in range(2):
            part = jnp.transpose(jnp.broadcast_to(value[h : h + 1, :], (128, 128)))
            twice[pl.ds(h * 128, 128), :] = part
            twice[pl.ds(rows + h * 128, 128), :] = part
        return twice[pl.ds(shift, rows), :]

    for copy in y_stats:
        copy.wait_recv()
    mine = stat_send[...]
    top, total, mixed, picked = merge([mine] + [stat_y[j] for j in range(1, NT)])
    group[0:2, :] = top
    group[2:4, :] = total
    group[4:6, :] = mixed
    group[6:8, :] = picked
    z_stats = []
    for d in Z_ORDER:
        z_stats.append(send(group, stat_z.at[d], at_pipe(d)))
    own[0] = spread(jnp.exp(mine[0:2] - top))
    own[1] = spread(jnp.exp(stat_y[1][0:2] - top))

    def add_core(dy, part):
        own_factor = jnp.concatenate([own[0, part, :]] * lanes, axis=1)
        core_factor = jnp.concatenate([own[1, part, :]] * lanes, axis=1)
        return term[dy, part, :] * own_factor + core_t[dy, part, :].astype(F32) * core_factor

    for pieces, _ in SUMS:
        for dy in Y_ORDER:
            if pieces[0][0] == SUMS[0][0][0][0]:
                t_core[dy].wait_recv()
            k = tensor_of(dy, 0)
            for first, number in pieces:
                part = slots(first, number)
                send_t[k, part, :] = add_core(dy, part).astype(BF16)
                t_y[dy, first] = send(send_t.at[k, part], y_t.at[dy - 1, part], at_tensor(dy, 0))
    t_core[0].wait_recv()
    for dy in cuts:
        o_y[dy].wait_recv()
    for pieces, _ in SUMS:
        for first, number in pieces:
            part = slots(first, number)
            target = send_o[t, part, :].astype(F32)
            for i in range(2):
                target = target + y_o[i, part, :].astype(F32)
            term[1, part, :] = target
            term[0, part, :] = add_core(0, part)
    for copy in z_stats:
        copy.wait_recv()
    group_top = group[0:2]
    top, total, mixed, picked = merge([group[...]] + [stat_z[d] for d in range(1, NZ)])
    full = total + jnp.exp(picked - top)
    loss_ref[...] = top + jnp.log(full) - picked
    own[0] = spread(jnp.exp(group_top - top) / full)
    own[1] = spread(total / full)
    own_dot = spread((mixed - total * picked) / full)[NEAR * BLK : (NEAR + 1) * BLK]
    z_grads = {}
    for pieces, offsets in SUMS:
        for first, number in pieces:
            part = slots(first, number)
            for dy in Y_ORDER:
                t_y[dy, first].wait_recv()
            value = term[0, part, :]
            for dy in range(NY - 1):
                value = value + y_t[dy, part, :].astype(F32)
            scale = jnp.concatenate([own[0, part, :]] * lanes, axis=1)
            drop = jnp.concatenate([own[1, part, :]] * lanes, axis=1)
            value = value * scale - term[1, part, :] * drop
            z_send[part, :] = value.astype(BF16)
            if first <= NEAR < first + number:
                term[2, slots(NEAR), :] = value[(NEAR - first) * BLK : (NEAR - first + 1) * BLK]
        for d in offsets:
            z_grads[d] = send(z_send.at[slots(slot_of(d))], z_recv.at[d], at_pipe(d))
    grad = term[2, slots(NEAR), :]
    for d in Z_ORDER:
        z_grads[d].wait_recv()
        grad = grad + z_recv[d].astype(F32)
    stream = tok_ref[...].astype(F32)
    weighted = grad * gain_of(t)
    dots = own_dot[:, :1] / (own_inv * (width * NT))
    grad_ref[...] = own_inv * (weighted - stream * (own_inv * own_inv * dots))
    for copy in started:
        copy.wait_send()


def hand_out(loss_ref, grad_ref, loss_out, grad_out):
    loss_out[...] = loss_ref[...]
    grad_out[...] = grad_ref[...]


def body(tokens, final_gain, unembed, targets):
    vocab, features = unembed.shape
    width = tokens.shape[1]
    rows = targets.shape[0]
    vmem = pl.BlockSpec(memory_space=pltpu.VMEM)
    results = (
        jax.ShapeDtypeStruct((2, 128), F32),
        jax.ShapeDtypeStruct(tokens.shape, F32),
    )
    loss, grad = pl.pallas_call(
        kernel,
        out_shape=results,
        in_specs=[vmem, vmem, vmem, pl.BlockSpec(memory_space=pl.ANY)],
        out_specs=(vmem, vmem),
        scratch_shapes=[
            pltpu.VMEM((NT, rows, width), BF16),
            pltpu.VMEM((NT, vocab, width), BF16),
            pltpu.VMEM((NT, vocab, width), BF16),
            pltpu.VMEM((rows, vocab), F32),
            pltpu.VMEM((rows, vocab), BF16),
            pltpu.VMEM((NY, rows, width), F32),
            pltpu.VMEM((NT, rows, width), BF16),
            pltpu.VMEM((NT, rows, width), BF16),
            pltpu.VMEM((NY, rows, width), BF16),
            pltpu.VMEM((NY, rows, width), BF16),
            pltpu.VMEM((NY - 1, rows, width), BF16),
            pltpu.VMEM((2, rows, width), BF16),
            pltpu.VMEM((2, rows, width // 2), BF16),
            pltpu.VMEM((2, rows, 128), F32),
            pltpu.VMEM((rows, width), BF16),
            pltpu.VMEM((NZ, BLK, width), BF16),
            pltpu.VMEM((8, 128), F32),
            pltpu.VMEM((NT, 8, 128), F32),
            pltpu.VMEM((8, 128), F32),
            pltpu.VMEM((NZ, 8, 128), F32),
            pltpu.VMEM((2 * rows, 128), F32),
            pltpu.VMEM((2 * rows, 128), jnp.int32),
            pltpu.SemaphoreType.DMA((NT + 1,)),
            pltpu.SemaphoreType.DMA((160,)),
            pltpu.SemaphoreType.DMA((160,)),
        ],
        compiler_params=pltpu.CompilerParams(
            collective_id=0, has_side_effects=True, vmem_limit_bytes=60 * 1024 * 1024
        ),
    )(tokens, final_gain.reshape(features // 128, 128), targets.reshape(2, 128), unembed)
    loss, grad = pl.pallas_call(
        hand_out, out_shape=results, in_specs=[vmem, vmem], out_specs=(vmem, vmem)
    )(loss, grad)
    return loss.reshape(rows), grad


def solution(mesh):
    placed = (P(("dp", "pipe"), "tensor"), P(), P(("tensor", "pipe"), None), P("dp"))
    return jax.shard_map(
        body,
        mesh=mesh,
        in_specs=placed,
        out_specs=(P("dp"), P(("dp", "pipe"), "tensor")),
        check_vma=False,
    )
```

```python
import functools

import jax
import jax.numpy as jnp
from jax import lax
from jax.experimental import pallas as pl
from jax.experimental.pallas import tpu as pltpu
from jax.sharding import PartitionSpec as P

EPS = 1e-06
MESH = pl.DeviceIdType.MESH
NY, NC, NZ = 4, 2, 16
NT = NY * NC
BLK = 16
F32, BF16 = jnp.float32, jnp.bfloat16
NEAR = 4
NEAR_SLOTS = 2 * NEAR + 1
GROUPS = [[(4, 1)], [(2, 2), (5, 2)], [(0, 2), (7, 2)], [(9, 2), (14, 2)], [(11, 3)]]
FAR_OFFSETS = [8, 7, 9, 6, 10, 5, 11]
NEAR_OFFSETS = [4, 12, 3, 13, 2, 14, 1, 15]
Z_ORDER = FAR_OFFSETS + NEAR_OFFSETS
Y_ORDER = [2, 1, 3]
SUMS = [([(11, 3)], FAR_OFFSETS[:3]), ([(9, 2), (14, 2)], FAR_OFFSETS[3:]), ([(0, 3), (6, 3)], NEAR_OFFSETS[:6]), ([(3, 3)], NEAR_OFFSETS[6:])]


def slot_of(offset):
    return (offset + NEAR) % NZ


def kernel(
    tok_ref, gain_ref, tgt_ref, u_hbm, loss_ref, grad_ref,
    xs, us, ug, logits, q, term, send_t, send_o, core_t, core_o, y_t, y_o, o_half, t_half, own, z_send, z_recv,
    stat_send, stat_y, group, stat_z, twice, twice_int, u_sem, send_sem, recv_sem,
):
    dp = lax.axis_index("dp")
    t = lax.axis_index("tensor")
    z = lax.axis_index("pipe")
    y, c = t // NC, t % NC
    rows = BLK * NZ
    near_rows = NEAR_SLOTS * BLK
    width = tok_ref.shape[1]
    lanes = width // 128
    vocab = us.shape[1]
    count = [0]
    started = []

    def tensor_of(dy, dc):
        return lax.rem(y + dy, NY) * NC + lax.rem(c + dc, NC)

    def at_tensor(dy, dc):
        return (dp, tensor_of(dy, dc), z)

    def at_pipe(d):
        return (dp, t, lax.rem(z + d, NZ))

    def send(src, dst, device):
        i = count[0]
        count[0] += 1
        copy = pltpu.make_async_remote_copy(
            src_ref=src, dst_ref=dst, send_sem=send_sem.at[i], recv_sem=recv_sem.at[i],
            device_id=device, device_id_type=MESH,
        )
        copy.start()
        started.append(copy)
        return copy

    def slots(first, number=1):
        return pl.ds(first * BLK, number * BLK)

    def gain_of(k):
        return jnp.concatenate([gain_ref[pl.ds(lanes * k + i, 1), :] for i in range(lanes)], axis=1)

    barrier = pltpu.get_barrier_semaphore()
    for d in range(1, NZ):
        pl.semaphore_signal(barrier, inc=1, device_id=at_pipe(d), device_id_type=MESH)
    for j in range(1, NT):
        pl.semaphore_signal(barrier, inc=1, device_id=at_tensor(j // NC, j % NC), device_id_type=MESH)

    loads = []
    for k in range(NT):
        load = pltpu.make_async_copy(u_hbm.at[:, pl.ds(k * width, width)], us.at[k], u_sem.at[k])
        load.start()
        loads.append(load)
    own_copy = pltpu.make_async_copy(tok_ref, xs.at[t, slots(NEAR)], u_sem.at[NT])
    own_copy.start()

    for h in range(2):
        part = jnp.transpose(jnp.broadcast_to(tgt_ref[h : h + 1, :], (128, 128)))
        twice_int[pl.ds(h * 128, 128), :] = part
        twice_int[pl.ds(rows + h * 128, 128), :] = part
    first_block = lax.rem(z + NZ - NEAR, NZ)
    shift = pl.multiple_of(first_block * BLK, BLK)
    back = pl.multiple_of(rows - first_block * BLK, BLK)
    vocab_start = (t * NZ + z) * vocab
    own_copy.wait()
    pl.semaphore_wait(barrier, NZ - 1 + NT - 1)

    z_copies = {}
    for d in NEAR_OFFSETS:
        z_copies[slot_of(NZ - d)] = send(tok_ref, xs.at[t, slots(slot_of(NZ - d))], at_pipe(d))
    y_copies, core_copies = [], [[] for _ in GROUPS]

    def forward(g):
        for first, number in GROUPS[g]:
            piece = xs.at[t, slots(first, number)]
            for dy in Y_ORDER:
                y_copies.append((g, dy, first, number, send(piece, piece, at_tensor(dy, 0))))
            core_copies[g].append(send(piece, piece, at_tensor(0, 1)))

    def hand_over(g):
        for group_of, dy, first, number, copy in y_copies:
            if group_of == g:
                copy.wait_recv()
                piece = xs.at[tensor_of(NY - dy, 0), slots(first, number)]
                core_copies[g].append(send(piece, piece, at_tensor(0, 1)))

    def wait_group(g):
        for first, number in GROUPS[g]:
            for s in range(first, first + number):
                if s != 0 and s != NEAR_SLOTS - 1:
                    z_copies[s].wait_recv()

    forward(0)
    for k in range(NT):
        loads[k].wait()
    lane = lax.broadcasted_iota(jnp.int32, (rows, vocab), 1)
    local = twice_int[pl.ds(shift, rows), :] - vocab_start
    local = jnp.concatenate([local] * ((vocab + 127) // 128), axis=1)[:, :vocab]
    q[...] = (lane == local).astype(F32).astype(BF16)
    o_core, o_y = {}, {}
    for dy in Y_ORDER:
        k = tensor_of(dy, 1)
        send_o[k] = jnp.dot(q[...], us[k], preferred_element_type=F32).astype(BF16)
        o_core[dy] = send(send_o.at[k], core_o.at[dy], at_tensor(0, 1))
    wait_group(1)
    forward(1)
    z_copies[0].wait_recv()
    z_copies[NEAR_SLOTS - 1].wait_recv()
    far_ahead = xs.at[t, slots(0)]
    far_behind = xs.at[t, slots(NEAR_SLOTS - 1)]
    across = xs.at[t, pl.ds(pl.multiple_of(c * ((NEAR_SLOTS - 1) * BLK), BLK), BLK)]
    z_copies[slot_of(8)] = send(across, xs.at[t, slots(slot_of(8))], at_pipe(NEAR + c * (NZ - 2 * NEAR)))
    for j in (1, 2, 3):
        z_copies[NZ - j] = send(far_ahead, xs.at[t, slots(NZ - j)], at_pipe(j))
        z_copies[NEAR_SLOTS - 1 + j] = send(far_behind, xs.at[t, slots(NEAR_SLOTS - 1 + j)], at_pipe(NZ - j))
    wait_group(2)
    forward(2)
    hand_over(0)
    for dy in (0,):
        k = tensor_of(dy, 1)
        send_o[k] = jnp.dot(q[...], us[k], preferred_element_type=F32).astype(BF16)
        o_core[dy] = send(send_o.at[k], core_o.at[dy], at_tensor(0, 1))

    half = width // 2
    cuts = {1: pl.ds(0, half), 3: pl.ds(half, half)}
    o_through = {}

    def sum_target(dy):
        k = tensor_of(dy, 0)
        total = jnp.dot(q[...], us[k], preferred_element_type=F32)
        o_core[dy].wait_recv()
        send_o[k] = (total + core_o[dy].astype(F32)).astype(BF16)
        if dy in cuts:
            o_through[dy].wait_recv()
            passing = o_half[dy // 2].astype(F32)
            send_o[k, :, cuts[dy]] = (send_o[k, :, cuts[dy]].astype(F32) + passing).astype(BF16)

    def send_target(dy):
        o_y[dy] = send(send_o.at[tensor_of(dy, 0)], y_o.at[dy // 2], at_tensor(dy, 0))

    sum_target(2)
    for dy in cuts:
        o_through[dy] = send(send_o.at[tensor_of(2, 0), :, cuts[dy]], o_half.at[dy // 2], at_tensor(dy, 0))
    hand_over(1)

    def scale_u(k, _):
        ug[k] = (us[k].astype(F32) * gain_of(k)).astype(BF16)
        return 0

    lax.fori_loop(0, NT, scale_u, 0)
    wait_group(3)
    forward(3)
    wait_group(4)
    forward(4)
    hand_over(2)

    def products(first, size):
        part = pl.ds(first, size)
        logits[part, :] = jnp.zeros((size, vocab), F32)

        def multiply(k, total):
            x = xs[k, part, :]
            logits[part, :] += lax.dot_general(x, ug[k], (((1,), (1,)), ((), ())), preferred_element_type=F32)
            xf = x.astype(F32)
            xf = xf * xf
            for i in range(lanes):
                total = total + xf[:, i * 128 : (i + 1) * 128]
            return total

        squares = lax.fori_loop(0, NT, multiply, jnp.zeros((size, 128), F32))
        return lax.rsqrt(jnp.sum(squares, axis=1, keepdims=True) / (width * NT) + EPS)

    def softmax(first, size, inv):
        lane_id = lax.broadcasted_iota(jnp.int32, (size, 128), 1)
        column = lax.broadcasted_iota(jnp.int32, (size, vocab), 1)
        part = pl.ds(first, size)
        l = logits[part, :] * inv
        tgt = twice_int[pl.ds(pl.multiple_of(shift + first, BLK), size), :][:, :1] - vocab_start
        here = column == tgt
        top = jnp.max(l, axis=1, keepdims=True)
        e = jnp.where(here, 0.0, jnp.exp(l - top))
        q[part, :] = e.astype(BF16)
        total = jnp.sum(e, axis=1, keepdims=True)
        mixed = jnp.sum(e * l, axis=1, keepdims=True)
        picked = jnp.sum(jnp.where(here, l, 0.0), axis=1, keepdims=True)
        stats = jnp.where(lane_id == 0, top, jnp.where(lane_id == 1, total, jnp.where(lane_id == 2, mixed, picked)))
        twice[part, :] = stats
        twice[pl.ds(rows + first, size), :] = stats

    for dy in Y_ORDER[1:] + [0]:
        sum_target(dy)
    for g in range(3):
        for copy in core_copies[g]:
            copy.wait_recv()
    inv = products(0, near_rows)
    own_inv = inv[NEAR * BLK : (NEAR + 1) * BLK]
    for first in range(0, near_rows, 48):
        softmax(first, 48, inv[first : first + 48])
    hand_over(3)
    hand_over(4)
    for dy in cuts:
        send_target(dy)
    for copy in core_copies[3] + core_copies[4]:
        copy.wait_recv()
    inv = products(near_rows, rows - near_rows)
    softmax(near_rows, 64, inv[:64])
    softmax(near_rows + 64, 48, inv[64:])
    for h in range(2):
        start = pl.multiple_of(back if h == 0 else lax.rem(back + 128, rows), BLK)
        turned = jnp.transpose(twice[pl.ds(start, 128), :])
        for i in range(4):
            stat_send[pl.ds(2 * i + h, 1), :] = turned[i : i + 1, :]
    y_stats = []
    for j in range(1, NT):
        y_stats.append(send(stat_send, stat_y.at[j], at_tensor(j // NC, j % NC)))

    t_core, t_y = {}, {}
    for dy in Y_ORDER + [0]:
        k = tensor_of(dy, 1)
        send_t[k] = jnp.dot(q[...], us[k], preferred_element_type=F32).astype(BF16)
        t_core[dy] = send(send_t.at[k], core_t.at[dy], at_tensor(0, 1))
    for dy in Y_ORDER + [0]:
        term[dy] = jnp.dot(q[...], us[tensor_of(dy, 0)], preferred_element_type=F32)

    def merge(tiles):
        top = tiles[0][0:2]
        for tile in tiles[1:]:
            top = jnp.maximum(top, tile[0:2])
        total = mixed = picked = jnp.zeros((2, 128), F32)
        for tile in tiles:
            factor = jnp.exp(tile[0:2] - top)
            total = total + factor * tile[2:4]
            mixed = mixed + factor * tile[4:6]
            picked = picked + tile[6:8]
        return top, total, mixed, picked

    def spread(value):
        for h in range(2):
            part = jnp.transpose(jnp.broadcast_to(value[h : h + 1, :], (128, 128)))
            twice[pl.ds(h * 128, 128), :] = part
            twice[pl.ds(rows + h * 128, 128), :] = part
        return twice[pl.ds(shift, rows), :]

    for copy in y_stats:
        copy.wait_recv()
    mine = stat_send[...]
    top, total, mixed, picked = merge([mine] + [stat_y[j] for j in range(1, NT)])
    group[0:2, :] = top
    group[2:4, :] = total
    group[4:6, :] = mixed
    group[6:8, :] = picked
    z_stats = []
    for d in Z_ORDER:
        z_stats.append(send(group, stat_z.at[d], at_pipe(d)))
    own[0] = spread(jnp.exp(mine[0:2] - top))
    own[1] = spread(jnp.exp(stat_y[1][0:2] - top))

    def add_core(dy, part):
        own_factor = jnp.concatenate([own[0, part, :]] * lanes, axis=1)
        core_factor = jnp.concatenate([own[1, part, :]] * lanes, axis=1)
        return term[dy, part, :] * own_factor + core_t[dy, part, :].astype(F32) * core_factor

    t_through = {}
    t_core[2].wait_recv()
    for pieces, _ in SUMS:
        for first, number in pieces:
            part = slots(first, number)
            send_t[tensor_of(2, 0), part, :] = add_core(2, part).astype(BF16)
            for dy in cuts:
                t_through[dy, first] = send(
                    send_t.at[tensor_of(2, 0), part, cuts[dy]], t_half.at[dy // 2, part], at_tensor(dy, 0)
                )
    for dy in cuts:
        t_core[dy].wait_recv()
    for pieces, _ in SUMS:
        for first, number in pieces:
            for dy in cuts:
                k = tensor_of(dy, 0)
                part = slots(first, number)
                value = add_core(dy, part)
                t_through[dy, first].wait_recv()
                passing = t_half[dy // 2, part, :].astype(F32)
                beside = jnp.zeros_like(passing)
                passing = jnp.concatenate([passing, beside] if dy == 1 else [beside, passing], axis=1)
                send_t[k, part, :] = (value + passing).astype(BF16)
                t_y[dy, first] = send(send_t.at[k, part], y_t.at[dy // 2, part], at_tensor(dy, 0))
    t_core[0].wait_recv()
    for dy in cuts:
        o_y[dy].wait_recv()
    for pieces, _ in SUMS:
        for first, number in pieces:
            part = slots(first, number)
            target = send_o[t, part, :].astype(F32)
            for i in range(2):
                target = target + y_o[i, part, :].astype(F32)
            term[1, part, :] = target
            term[0, part, :] = add_core(0, part)
    for copy in z_stats:
        copy.wait_recv()
    group_top = group[0:2]
    top, total, mixed, picked = merge([group[...]] + [stat_z[d] for d in range(1, NZ)])
    full = total + jnp.exp(picked - top)
    loss_ref[...] = top + jnp.log(full) - picked
    own[0] = spread(jnp.exp(group_top - top) / full)
    own[1] = spread(total / full)
    own_dot = spread((mixed - total * picked) / full)[NEAR * BLK : (NEAR + 1) * BLK]
    z_grads = {}
    for pieces, offsets in SUMS:
        for first, number in pieces:
            part = slots(first, number)
            for dy in cuts:
                t_y[dy, first].wait_recv()
            value = term[0, part, :]
            for i in range(2):
                value = value + y_t[i, part, :].astype(F32)
            scale = jnp.concatenate([own[0, part, :]] * lanes, axis=1)
            drop = jnp.concatenate([own[1, part, :]] * lanes, axis=1)
            value = value * scale - term[1, part, :] * drop
            z_send[part, :] = value.astype(BF16)
            if first <= NEAR < first + number:
                term[2, slots(NEAR), :] = value[(NEAR - first) * BLK : (NEAR - first + 1) * BLK]
        for d in offsets:
            z_grads[d] = send(z_send.at[slots(slot_of(d))], z_recv.at[d], at_pipe(d))
    grad = term[2, slots(NEAR), :]
    for d in Z_ORDER:
        z_grads[d].wait_recv()
        grad = grad + z_recv[d].astype(F32)
    stream = tok_ref[...].astype(F32)
    weighted = grad * gain_of(t)
    dots = own_dot[:, :1] / (own_inv * (width * NT))
    grad_ref[...] = own_inv * (weighted - stream * (own_inv * own_inv * dots))
    for copy in started:
        copy.wait_send()


def hand_out(loss_ref, grad_ref, loss_out, grad_out):
    loss_out[...] = loss_ref[...]
    grad_out[...] = grad_ref[...]


def body(tokens, final_gain, unembed, targets):
    vocab, features = unembed.shape
    width = tokens.shape[1]
    rows = targets.shape[0]
    vmem = pl.BlockSpec(memory_space=pltpu.VMEM)
    results = (
        jax.ShapeDtypeStruct((2, 128), F32),
        jax.ShapeDtypeStruct(tokens.shape, F32),
    )
    loss, grad = pl.pallas_call(
        kernel,
        out_shape=results,
        in_specs=[vmem, vmem, vmem, pl.BlockSpec(memory_space=pl.ANY)],
        out_specs=(vmem, vmem),
        scratch_shapes=[
            pltpu.VMEM((NT, rows, width), BF16),
            pltpu.VMEM((NT, vocab, width), BF16),
            pltpu.VMEM((NT, vocab, width), BF16),
            pltpu.VMEM((rows, vocab), F32),
            pltpu.VMEM((rows, vocab), BF16),
            pltpu.VMEM((NY, rows, width), F32),
            pltpu.VMEM((NT, rows, width), BF16),
            pltpu.VMEM((NT, rows, width), BF16),
            pltpu.VMEM((NY, rows, width), BF16),
            pltpu.VMEM((NY, rows, width), BF16),
            pltpu.VMEM((2, rows, width), BF16),
            pltpu.VMEM((2, rows, width), BF16),
            pltpu.VMEM((2, rows, width // 2), BF16),
            pltpu.VMEM((2, rows, width // 2), BF16),
            pltpu.VMEM((2, rows, 128), F32),
            pltpu.VMEM((rows, width), BF16),
            pltpu.VMEM((NZ, BLK, width), BF16),
            pltpu.VMEM((8, 128), F32),
            pltpu.VMEM((NT, 8, 128), F32),
            pltpu.VMEM((8, 128), F32),
            pltpu.VMEM((NZ, 8, 128), F32),
            pltpu.VMEM((2 * rows, 128), F32),
            pltpu.VMEM((2 * rows, 128), jnp.int32),
            pltpu.SemaphoreType.DMA((NT + 1,)),
            pltpu.SemaphoreType.DMA((160,)),
            pltpu.SemaphoreType.DMA((160,)),
        ],
        compiler_params=pltpu.CompilerParams(
            collective_id=0, has_side_effects=True, vmem_limit_bytes=60 * 1024 * 1024
        ),
    )(tokens, final_gain.reshape(features // 128, 128), targets.reshape(2, 128), unembed)
    loss, grad = pl.pallas_call(
        hand_out, out_shape=results, in_specs=[vmem, vmem], out_specs=(vmem, vmem)
    )(loss, grad)
    return loss.reshape(rows), grad


def solution(mesh):
    placed = (P(("dp", "pipe"), "tensor"), P(), P(("tensor", "pipe"), None), P("dp"))
    return jax.shard_map(
        body,
        mesh=mesh,
        in_specs=placed,
        out_specs=(P("dp"), P(("dp", "pipe"), "tensor")),
        check_vma=False,
    )
```
